256 devices in a mesh: lon: 16 (over z, core), lat: 16 (over y, x).
Axes of the slice: x: 4, y: 4, z: 8, core: 2. Of those that a mesh axis runs over, the one named last changes fastest.
Arguments:
- background: bfloat16 [64, 16, 256, 2048], P(None, None, 'lat', 'lon'), may hold values from -6 to 6
- ocean: int32 [256, 2048], P('lat', 'lon'), may hold values 0 or 1
- obs_level: int32 [16, 16, 2048], P('lat', 'lon'), may hold values from 0 to 15
- obs_row: int32 [16, 16, 2048], P('lat', 'lon'), may hold values from 0 to 16
- obs_col: int32 [16, 16, 2048], P('lat', 'lon'), may hold values from 0 to 128
- frac_row: float32 [16, 16, 2048], P('lat', 'lon'), may hold values from 0 to 1
- frac_col: float32 [16, 16, 2048], P('lat', 'lon'), may hold values from 0 to 1
- obs_value: float32 [16, 16, 2048], P('lat', 'lon'), may hold values from -8 to 8
- obs_error: float32 [16, 16, 2048], P('lat', 'lon'), may hold values from 1 to 10
- obs_flag: int32 [16, 16, 2048], P('lat', 'lon'), may hold values 0 or 1
Outputs:
- analysis: bfloat16 [64, 16, 256, 2048], P(None, None, 'lat', 'lon')
- departure: float32 [16, 16, 2048], P('lat', 'lon')
The draws below stay inside these ranges and needn't reach their ends.
All inputs are finite; a program needn't handle non-finite values. No bound on the sum of `ocean` or of `obs_flag` on one device may be relied on, other than what follows from the above.
Results may differ from the reference program's by a relative error of at most 0.005.
Values may be sent and summed in bfloat16 or wider, within the bound.
A program may use at most 64 MiB of HBM per device.

```python
import math
import jax
import jax.numpy as jnp
from jax import lax

MEMBERS = 64
LEVELS = 16
CY = 16
CX = 128
NOBS = 2048
NS_ITERS = 6
NY = 256
NX = 2048
N_LON = 16
N_LAT = 16


def set_ends(values, own_key, low, high):
    longest = values.shape.index(max(values.shape))
    spots = []
    for shift in (0, 1):
        where = [jax.random.randint(jax.random.fold_in(own_key, axis), (), 0, length) for axis, length in enumerate(values.shape)]
        where[longest] = (where[longest] + shift) % values.shape[longest]
        spots.append(tuple(where))
    return values.at[spots[0]].set(low).at[spots[1]].set(high)


def steps_of(stream_key, dims, pieces, least, high):
    factor_of, own = 1.0, jax.random.fold_in(stream_key, 6)
    for position, parts in pieces:
        steps = jnp.exp(jax.random.uniform(jax.random.fold_in(own, position), (parts,), jnp.float32, least / len(pieces), high / len(pieces)))
        factor_of = factor_of * jnp.repeat(steps, dims[position] // parts).reshape([-1 if axis == position else 1 for axis in range(len(dims))])
    return factor_of


def normal_values(own_key, dims, width, reach, pieces=(), kind=jnp.bfloat16):
    entries = width * jax.random.normal(own_key, dims, jnp.float32)
    if pieces:
        entries = entries * steps_of(own_key, dims, pieces, -0.22, 0.18)
    return jnp.clip(entries, -reach, reach).astype(kind)


def setup_inputs(seed: int = 0) -> dict:
    keys = jax.random.split(jax.random.key(seed), 11)
    return {
        "background": normal_values(keys[0], (MEMBERS, LEVELS, NY, NX), 1.0, 6.0, ((2, 16), (3, 16))),
        "ocean": set_ends((jax.random.randint(keys[1], (NY, NX), 0, 4) < 3).astype(jnp.int32), jax.random.fold_in(keys[1], 1), 0, 1),
        "obs_level": set_ends(jax.random.randint(keys[2], (N_LAT, N_LON, NOBS), 0, LEVELS), jax.random.fold_in(keys[2], 1), 0, LEVELS - 1).astype(jnp.int32),
        "obs_row": set_ends(jax.random.randint(keys[3], (N_LAT, N_LON, NOBS), 0, CY + 1), jax.random.fold_in(keys[3], 1), 0, CY).astype(jnp.int32),
        "obs_col": set_ends(jax.random.randint(keys[4], (N_LAT, N_LON, NOBS), 0, CX + 1), jax.random.fold_in(keys[4], 1), 0, CX).astype(jnp.int32),
        "frac_row": jnp.clip(1.0 * jax.random.uniform(keys[5], (N_LAT, N_LON, NOBS), jnp.float32) ** steps_of(keys[5], (N_LAT, N_LON, NOBS), ((0, 16), (1, 16)), -0.2, 0.2), 0.0, 1.0),
        "frac_col": jnp.clip(1.0 * jax.random.uniform(keys[6], (N_LAT, N_LON, NOBS), jnp.float32) ** steps_of(keys[6], (N_LAT, N_LON, NOBS), ((0, 16), (1, 16)), -0.2, 0.2), 0.0, 1.0),
        "obs_value": normal_values(keys[7], (N_LAT, N_LON, NOBS), 1.5, 8.0, ((0, 16), (1, 16)), jnp.float32),
        "obs_error": jnp.clip(jnp.exp(math.log(10.0) - 2.3025851 * jax.random.uniform(keys[8], (N_LAT, N_LON, NOBS), jnp.float32) ** steps_of(keys[8], (N_LAT, N_LON, NOBS), ((0, 16), (1, 16)), -0.2, 0.2)), 1.0, 10.0),
        "obs_flag": set_ends((jax.random.randint(keys[9], (N_LAT, N_LON, NOBS), 0, 8) < 7).astype(jnp.int32), jax.random.fold_in(keys[9], 1), 0, 1),
    }


inflation = 1.2
highest = lax.Precision.HIGHEST

def reference(background, ocean, obs_level, obs_row, obs_col, frac_row, frac_col, obs_value, obs_error, obs_flag):
    height = CY * N_LAT
    breadth = CX * N_LON
    flat = background.reshape(MEMBERS, -1)
    lat_base = (jnp.arange(N_LAT, dtype=jnp.int32) * CY)[:, None, None]
    lon_base = (jnp.arange(N_LON, dtype=jnp.int32) * CX)[None, :, None]

    def corner(down, right):
        rows = lat_base + obs_row - 1 + down
        cols = (lon_base + obs_col - 1 + right) % breadth
        inside = ((rows >= 0) & (rows < height)).astype(jnp.float32)
        spot = (obs_level * height + jnp.clip(rows, 0, height - 1)) * breadth + cols
        vals = jnp.take(flat, spot.reshape(-1).astype(jnp.int32), axis=1).astype(jnp.float32)
        return vals.reshape(MEMBERS, N_LAT, N_LON, NOBS) * inside
    model_obs = (1.0 - frac_row) * (1.0 - frac_col) * corner(0, 0) + (1.0 - frac_row) * frac_col * corner(0, 1) + frac_row * (1.0 - frac_col) * corner(1, 0) + frac_row * frac_col * corner(1, 1)
    obs_mean = lax.optimization_barrier(jnp.mean(model_obs, axis=0))
    obs_pert = (model_obs - obs_mean).astype(jnp.bfloat16)
    innov = obs_value - obs_mean
    flag = obs_flag.astype(jnp.float32)
    departure = flag * innov
    info = jnp.stack([innov, flag / obs_error, obs_col.astype(jnp.float32) - 0.5 + frac_col - CX / 2, obs_row.astype(jnp.float32) - 0.5 + frac_row - CY / 2]).astype(jnp.bfloat16).astype(jnp.float32)
    cross = jnp.zeros((N_LAT, N_LON, MEMBERS, MEMBERS), jnp.float32)
    drive = jnp.zeros((N_LAT, N_LON, MEMBERS), jnp.float32)
    lat_index = jnp.arange(N_LAT, dtype=jnp.int32)[:, None, None]
    for shift_lon in (-1, 0, 1):
        for shift_lat in (-1, 0, 1):
            moved_pert = jnp.roll(jnp.roll(obs_pert, shift_lat, axis=1), shift_lon, axis=2)
            moved_info = jnp.roll(jnp.roll(info, shift_lat, axis=1), shift_lon, axis=2)
            source = lat_index - shift_lat
            present = ((source >= 0) & (source < N_LAT)).astype(jnp.float32)
            along = (moved_info[2] - shift_lon * CX) / CX
            across = (moved_info[3] - shift_lat * CY) / CY
            weight = moved_info[1] * present * jnp.exp(-0.5 * (along * along + across * across))
            weighted = (moved_pert.astype(jnp.float32) * weight).astype(jnp.bfloat16).astype(jnp.float32)
            cross = cross + jnp.einsum('kpqo,lpqo->pqkl', weighted, moved_pert.astype(jnp.float32), precision=highest)
            drive = drive + jnp.einsum('kpqo,pqo->pqk', weighted, moved_info[0] * present, precision=highest)
    eye = jnp.eye(MEMBERS, dtype=jnp.float32)
    system = (MEMBERS - 1) / inflation * eye + cross
    scale = jnp.sqrt(lax.optimization_barrier(jnp.sum(system * system, axis=(-2, -1))))[..., None, None]
    upper = system / scale
    lower = jnp.broadcast_to(eye, system.shape)
    for step in range(NS_ITERS):
        middle = 1.5 * eye - 0.5 * jnp.einsum('pqij,pqjk->pqik', lower, upper, precision=highest)
        upper = jnp.einsum('pqij,pqjk->pqik', upper, middle, precision=highest)
        lower = jnp.einsum('pqij,pqjk->pqik', middle, lower, precision=highest)
    root = lower / jnp.sqrt(scale)
    inverse = jnp.einsum('pqij,pqjk->pqik', root, root, precision=highest)
    mean_weights = jnp.einsum('pqjk,pqk->pqj', inverse, drive, precision=highest)
    transform = (math.sqrt(MEMBERS - 1) * root + mean_weights[..., None]).astype(jnp.bfloat16)

    def apply_row(index, result):
        start = (index * CY).astype(jnp.int32)
        slab = lax.dynamic_slice_in_dim(background, start, CY, 2).astype(jnp.float32)
        slab = slab.reshape(MEMBERS, LEVELS, CY, N_LON, CX)
        bg_mean = lax.optimization_barrier(jnp.mean(slab, axis=0))
        spread = (slab - bg_mean).astype(jnp.bfloat16).astype(jnp.float32)
        row_transform = lax.dynamic_index_in_dim(transform, index, 0, keepdims=False).astype(jnp.float32)
        update = jnp.einsum('qjk,jlyqx->klyqx', row_transform, spread, precision=highest)
        land = lax.dynamic_slice_in_dim(ocean, start, CY, 0).reshape(CY, N_LON, CX)
        mixed = jnp.where(land[None, None] > 0, bg_mean + update, slab)
        mixed = mixed.reshape(MEMBERS, LEVELS, CY, breadth).astype(jnp.bfloat16)
        return lax.dynamic_update_slice_in_dim(result, mixed, start, 2)
    analysis = lax.fori_loop(0, N_LAT, apply_row, jnp.zeros_like(background))
    return (analysis, departure)
```

```python
import functools
import math

import jax
import jax.numpy as jnp
from jax import lax
from jax.experimental import pallas as pl
from jax.experimental.pallas import tpu as pltpu
from jax.sharding import PartitionSpec as P

NS_ITERS = 6
INFLATION = 1.2

f32 = jnp.float32
bf16 = jnp.bfloat16
MESH = pl.DeviceIdType.MESH
SHIFTS = (-1, 0, 1)


def iota(shape, axis):
    return lax.broadcasted_iota(jnp.int32, shape, axis)


def dot(a, b):
    return jnp.dot(a, b, precision=lax.Precision.HIGHEST, preferred_element_type=f32)


def dot_t(a, b):
    return lax.dot_general(a, b, (((1,), (1,)), ((), ())), preferred_element_type=f32)


def observe(
    n_lon,
    n_lat,
    background,
    spot_any,
    row,
    col,
    frac_row,
    frac_col,
    value,
    error,
    flag,
    sums_out,
    departure,
    held,
    stage,
    edge,
    edge_in,
    table,
    side,
    side_in,
    spot,
    picked,
    pert,
    weighted,
    own,
    lon_in,
    lat_out,
    lat_in,
    load_sem,
    spot_sem,
    edge_send,
    edge_recv,
    side_send,
    side_recv,
    lon_send,
    lon_recv,
    lat_send,
    lat_recv,
):
    members, levels, depth, width = background.shape
    observations = spot.shape[0]
    stride = width + 8
    first = 8
    pairs = depth + 1
    at_lon, at_lat = lax.axis_index("lon"), lax.axis_index("lat")
    lon_at = {d: (lax.rem(at_lon + d + n_lon, n_lon), at_lat) for d in (-1, 1)}
    lat_at = {d: (at_lon, lax.rem(at_lat + d + n_lat, n_lat)) for d in (-1, 1)}

    chunks = load_sem.shape[0]
    each = levels // chunks
    loads = [
        pltpu.make_async_copy(
            background.at[:, pl.ds(c * each, each)],
            held.at[:, pl.ds(c * each, each)],
            load_sem.at[c],
        )
        for c in range(chunks)
    ]
    for load in loads:
        load.start()
    spot_load = pltpu.make_async_copy(spot_any, spot, spot_sem)
    spot_load.start()

    barrier = pltpu.get_barrier_semaphore()
    for there in (lon_at[-1], lon_at[1], lat_at[-1], lat_at[1]):
        pl.semaphore_signal(barrier, inc=1, device_id=there, device_id_type=MESH)
    pl.semaphore_wait(barrier, 4)

    def place(pair, level):
        return pl.multiple_of((pair * levels + level) * stride + first, 8)

    def turned(upper, lower):
        return jnp.concatenate([upper, lower], axis=0).astype(bf16).T.astype(f32)

    def build(level, carry):
        stage[...] = held[:, level].astype(f32).reshape(members * depth, width)
        rows = [stage[pl.ds(r, members, stride=depth), :] for r in range(depth)]
        here = pl.ds(pl.multiple_of(level * members, members), members)
        edge[0, here, :] = rows[0].astype(bf16)
        edge[1, here, :] = rows[depth - 1].astype(bf16)
        for pair in range(1, depth):
            table[pl.ds(place(pair, level), width), :] = turned(rows[pair - 1], rows[pair])
        return carry

    part = each * members
    edge_copies = []
    for c in range(chunks):
        loads[c].wait()
        lax.fori_loop(c * each, (c + 1) * each, build, 0)
        for index, toward in ((0, -1), (1, 1)):
            copy = pltpu.make_async_remote_copy(
                src_ref=edge.at[index, pl.ds(c * part, part)],
                dst_ref=edge_in.at[1 - index, pl.ds(c * part, part)],
                send_sem=edge_send.at[index, c],
                recv_sem=edge_recv.at[1 - index, c],
                device_id=lat_at[toward],
                device_id_type=MESH,
            )
            copy.start()
            edge_copies.append(copy)

    def side_copy(index, toward, begin, count, slot):
        return pltpu.make_async_remote_copy(
            src_ref=side.at[index, pl.ds(begin, count)],
            dst_ref=side_in.at[1 - index, pl.ds(begin, count)],
            send_sem=side_send.at[index, slot],
            recv_sem=side_recv.at[1 - index, slot],
            device_id=lon_at[toward],
            device_id_type=MESH,
        )

    total = pairs * levels
    inner = (depth - 1) * levels
    spans = ((levels, inner, levels, 0), (0, levels, 0, 1), (depth * levels, levels, depth * levels, 2))

    def send_sides(span):
        begin, count, _, slot = span
        copies = []
        for index, edge_col, toward in ((0, 0, -1), (1, width - 1, 1)):
            side[index, begin : begin + count, :] = table[
                pl.ds(begin * stride + first + edge_col, count, stride=stride), :
            ].astype(bf16)
            copy = side_copy(index, toward, begin, count, slot)
            copy.start()
            copies.append(copy)
        return copies

    side_copies = send_sides(spans[0])

    for copy in edge_copies:
        copy.wait()
    top = jnp.where(at_lat > 0, 1.0, 0.0).astype(f32)
    bottom = jnp.where(at_lat < n_lat - 1, 1.0, 0.0).astype(f32)

    def build_edges(level, carry):
        here = pl.ds(pl.multiple_of(level * members, members), members)
        north = edge_in[0, here, :].astype(f32) * top
        south = edge_in[1, here, :].astype(f32) * bottom
        table[pl.ds(place(0, level), width), :] = turned(north, edge[0, here, :].astype(f32))
        table[pl.ds(place(depth, level), width), :] = turned(edge[1, here, :].astype(f32), south)
        return carry

    lax.fori_loop(0, levels, build_edges, 0)
    side_copies += send_sides(spans[1]) + send_sides(spans[2])
    spot_load.wait()
    for copy in side_copies:
        copy.wait()
    table[pl.ds(first - 1, total, stride=stride), :] = side_in[0].astype(f32)
    table[pl.ds(stride, total, stride=stride), :] = side_in[1].astype(f32)

    def pick(o, carry):
        picked[pl.ds(o * 2, 2), :] = table[pl.ds(spot[o], 2), :]
        return carry

    lax.fori_loop(0, observations, pick, 0, unroll=16)

    pert[members:, :] = jnp.zeros((pert.shape[0] - members, observations), bf16)
    lanes = 128

    def block(b, carry):
        start = pl.multiple_of(b * lanes, lanes)
        here = pl.ds(start, lanes)
        corners = [
            picked[pl.ds(start * 2 + s, lanes, stride=2), :].astype(bf16).T.astype(f32)
            for s in range(2)
        ]
        fr, fc = frac_row[:, here], frac_col[:, here]
        model = (
            (1.0 - fr) * (1.0 - fc) * corners[0][:members]
            + (1.0 - fr) * fc * corners[1][:members]
            + fr * (1.0 - fc) * corners[0][members:]
            + fr * fc * corners[1][members:]
        )
        mean = jnp.sum(model, axis=0, keepdims=True) * (1.0 / members)
        rounded = (model - mean).astype(bf16)
        pert[:members, here] = rounded
        innov = value[:, here] - mean
        flags = flag[:, here].astype(f32)
        departure[:, here] = flags * innov
        pert[members : members + 16, here] = jnp.where(iota((16, lanes), 0) == 0, innov, 0.0).astype(
            bf16
        )
        gain = (flags / error[:, here]).astype(bf16).astype(f32)
        along = (col[:, here].astype(f32) - 0.5 + fc - width / 2).astype(bf16).astype(f32)
        across = (row[:, here].astype(f32) - 0.5 + fr - depth / 2).astype(bf16).astype(f32)
        values = rounded.astype(f32)
        for a in range(3):
            u = (along - SHIFTS[a] * width) / width
            for c in range(3):
                w = (across - SHIFTS[c] * depth) / depth
                weight = gain * jnp.exp(-0.5 * (u * u + w * w))
                weighted[a, c * members : (c + 1) * members, here] = (values * weight).astype(bf16)
        return carry

    lax.fori_loop(0, observations // lanes, block, 0)

    lon_copies = []
    for a, index, toward in ((0, 0, -1), (2, 1, 1)):
        own[a] = dot_t(weighted[a], pert[...])
        copy = pltpu.make_async_remote_copy(
            src_ref=own.at[a],
            dst_ref=lon_in.at[1 - index],
            send_sem=lon_send.at[index],
            recv_sem=lon_recv.at[1 - index],
            device_id=lon_at[toward],
            device_id_type=MESH,
        )
        copy.start()
        lon_copies.append(copy)
    middle = dot_t(weighted[1], pert[...])
    for copy in lon_copies:
        copy.wait()
    summed = middle + lon_in[0] + lon_in[1]
    lat_copies = []
    for c, index, toward in ((0, 0, -1), (2, 1, 1)):
        lat_out[index] = summed[c * members : (c + 1) * members]
        copy = pltpu.make_async_remote_copy(
            src_ref=lat_out.at[index],
            dst_ref=lat_in.at[1 - index],
            send_sem=lat_send.at[index],
            recv_sem=lat_recv.at[1 - index],
            device_id=lat_at[toward],
            device_id_type=MESH,
        )
        copy.start()
        lat_copies.append(copy)
    for copy in lat_copies:
        copy.wait()
    sums_out[...] = summed[members : 2 * members] + lat_in[0] * top + lat_in[1] * bottom


def transform_of(sums, members):
    eye = (iota((members, members), 0) == iota((members, members), 1)).astype(f32)
    system = (members - 1) / INFLATION * eye + sums[:, :members]
    squares = jnp.sum(system * system, axis=0, keepdims=True)
    scale = jnp.sqrt(jnp.sum(squares, axis=1, keepdims=True))
    upper = system / scale
    middle = 1.5 * eye - 0.5 * upper
    both = jnp.concatenate([dot(upper, middle), middle], axis=0)
    for step in range(1, NS_ITERS):
        middle = 1.5 * eye - 0.5 * dot(both[members:], both[:members])
        if step < NS_ITERS - 1:
            both = dot(both, middle)
        else:
            lower = dot(both[members:], middle)
    root = lower / jnp.sqrt(scale)
    mean_weights = dot(root, dot(root, sums))[:, members : members + 1]
    return (math.sqrt(members - 1) * root + mean_weights).astype(bf16)


def update(
    sums, ocean, departure, background, analysis, departure_out, held, result, spread_by, load_sem, store_sem
):
    members, levels, depth, width = background.shape
    n = members * depth
    chunks = load_sem.shape[0]
    each = levels // chunks
    loads = [
        pltpu.make_async_copy(
            background.at[:, pl.ds(c * each, each)],
            held.at[:, pl.ds(c * each, each)],
            load_sem.at[c],
        )
        for c in range(chunks)
    ]
    for load in loads:
        load.start()
    departure_out[...] = departure[...]
    transform = transform_of(sums[...], members)
    shift = depth.bit_length() - 1
    down = (jnp.right_shift(iota((n, members), 0), shift) == iota((n, members), 1)).astype(f32)
    along = (jnp.right_shift(iota((members, n), 1), shift) == iota((members, n), 0)).astype(f32)
    tall = dot_t(down.astype(bf16), transform).astype(bf16)
    part = 256
    for b in range(n // part):
        wide = jnp.dot(
            tall[b * part : (b + 1) * part], along.astype(bf16), preferred_element_type=f32
        )
        same = jnp.bitwise_and(iota((part, n), 0) - iota((part, n), 1), depth - 1) == 0
        spread_by[b * part : (b + 1) * part, :] = jnp.where(same, wide, 0.0).astype(bf16)
    for load in loads:
        load.wait()
    water = ocean[...] > 0
    at_once = 2

    def store(step):
        span = pl.ds(step * at_once, at_once)
        return pltpu.make_async_copy(result.at[:, span], analysis.at[:, span], store_sem.at[step])

    def levels_of(step, carry):
        base = step * at_once
        states = [held[:, base + j].astype(f32) for j in range(at_once)]
        means = [jnp.sum(state, axis=0) * (1.0 / members) for state in states]
        spread = jnp.concatenate(
            [(s - m[None]).astype(bf16).reshape(n, width) for s, m in zip(states, means)], axis=1
        )
        for b in range(n // part):
            mixed = jnp.dot(
                spread_by[b * part : (b + 1) * part, :], spread, preferred_element_type=f32
            )
            some = slice(b * (part // depth), (b + 1) * (part // depth))
            for j in range(at_once):
                change = mixed[:, j * width : (j + 1) * width].reshape(part // depth, depth, width)
                result[some, base + j] = jnp.where(
                    water[None], means[j][None] + change, held[some, base + j].astype(f32)
                ).astype(bf16)
        store(step).start()
        return carry

    lax.fori_loop(0, levels // at_once, levels_of, 0)
    for step in range(levels // at_once):
        store(step).wait()


def on_device(
    n_lon,
    n_lat,
    background,
    ocean,
    obs_level,
    obs_row,
    obs_col,
    frac_row,
    frac_col,
    obs_value,
    obs_error,
    obs_flag,
):
    members, levels, depth, width = background.shape
    observations = obs_level.shape[-1]
    stride = width + 8
    total = (depth + 1) * levels
    chunks = 4
    level, row, col = (x.reshape(-1) for x in (obs_level, obs_row, obs_col))
    spot = (row * levels + level) * stride + 7 + col
    lines = [
        x.reshape(1, observations)
        for x in (obs_row, obs_col, frac_row, frac_col, obs_value, obs_error, obs_flag)
    ]
    vmem = pl.BlockSpec(memory_space=pltpu.VMEM)
    anywhere = pl.BlockSpec(memory_space=pl.ANY)
    dma = pltpu.SemaphoreType.DMA
    sums, departure = pl.pallas_call(
        functools.partial(observe, n_lon, n_lat),
        out_shape=(
            jax.ShapeDtypeStruct((members, 128), f32),
            jax.ShapeDtypeStruct((1, observations), f32),
        ),
        in_specs=[anywhere, anywhere] + [vmem] * 7,
        out_specs=(vmem, vmem),
        scratch_shapes=[
            pltpu.VMEM(background.shape, bf16),
            pltpu.VMEM((members * depth, width), f32),
            pltpu.VMEM((2, levels * members, width), bf16),
            pltpu.VMEM((2, levels * members, width), bf16),
            pltpu.VMEM((total * stride + 8, 2 * members), f32),
            pltpu.VMEM((2, total, 2 * members), bf16),
            pltpu.VMEM((2, total, 2 * members), bf16),
            pltpu.SMEM((observations,), jnp.int32),
            pltpu.VMEM((2 * observations, 2 * members), f32),
            pltpu.VMEM((128, observations), bf16),
            pltpu.VMEM((3, 3 * members, observations), bf16),
            pltpu.VMEM((3, 3 * members, 128), f32),
            pltpu.VMEM((2, 3 * members, 128), f32),
            pltpu.VMEM((2, members, 128), f32),
            pltpu.VMEM((2, members, 128), f32),
            dma((chunks,)),
            dma,
            dma((2, chunks)),
            dma((2, chunks)),
            dma((2, 3)),
            dma((2, 3)),
            dma((2,)),
            dma((2,)),
            dma((2,)),
            dma((2,)),
        ],
        compiler_params=pltpu.CompilerParams(
            collective_id=0, has_side_effects=True, vmem_limit_bytes=48 << 20
        ),
        name="observe",
    )(background, spot, *lines)
    n = members * depth
    analysis, departure = pl.pallas_call(
        update,
        out_shape=(
            jax.ShapeDtypeStruct(background.shape, bf16),
            jax.ShapeDtypeStruct(departure.shape, f32),
        ),
        in_specs=[vmem, vmem, vmem, anywhere],
        out_specs=(anywhere, vmem),
        scratch_shapes=[
            pltpu.VMEM(background.shape, bf16),
            pltpu.VMEM(background.shape, bf16),
            pltpu.VMEM((n, n), bf16),
            dma((chunks,)),
            dma((levels // 2,)),
        ],
        compiler_params=pltpu.CompilerParams(vmem_limit_bytes=40 << 20),
        name="update",
    )(sums, ocean, departure, background)
    return analysis, departure.reshape(obs_value.shape)


def solution(mesh):
    here = P("lat", "lon", None)
    in_specs = (P(None, None, "lat", "lon"), P("lat", "lon")) + (here,) * 8
    out_specs = (P(None, None, "lat", "lon"), here)
    return jax.shard_map(
        functools.partial(on_device, mesh.shape["lon"], mesh.shape["lat"]),
        mesh=mesh,
        in_specs=in_specs,
        out_specs=out_specs,
        check_vma=False,
    )
```

```python
import functools
import math

import jax
import jax.numpy as jnp
from jax import lax
from jax.experimental import pallas as pl
from jax.experimental.pallas import tpu as pltpu
from jax.sharding import PartitionSpec as P

NS_ITERS = 6
INFLATION = 1.2

f32 = jnp.float32
bf16 = jnp.bfloat16
MESH = pl.DeviceIdType.MESH
SHIFTS = (-1, 0, 1)


def iota(shape, axis):
    return lax.broadcasted_iota(jnp.int32, shape, axis)


def dot(a, b):
    return jnp.dot(a, b, precision=lax.Precision.HIGHEST, preferred_element_type=f32)


def dot_t(a, b):
    return lax.dot_general(a, b, (((1,), (1,)), ((), ())), preferred_element_type=f32)


def observe(
    n_lon,
    n_lat,
    background,
    level_in,
    row_in,
    col_in,
    frac_row_in,
    frac_col_in,
    value_in,
    error_in,
    flag_in,
    sums_out,
    departure,
    level,
    row,
    col,
    frac_row,
    frac_col,
    value,
    error,
    flag,
    spots,
    held,
    stage,
    edge,
    edge_in,
    table,
    side,
    side_in,
    corner_in,
    spot,
    picked,
    pert,
    weighted,
    own,
    sums_in,
    load_sem,
    line_sem,
    spot_sem,
    edge_send,
    edge_recv,
    side_send,
    side_recv,
    corner_send,
    corner_recv,
    sums_send,
    sums_recv,
):
    members, levels, depth, width = background.shape
    observations = spot.shape[1]
    stride = width + 8
    first = 8
    at_lon, at_lat = lax.axis_index("lon"), lax.axis_index("lat")

    def beside(lat, lon):
        return (lax.rem(at_lon + lon + n_lon, n_lon), lax.rem(at_lat + lat + n_lat, n_lat))

    def send(source, target, send_sem, recv_sem, lat, lon):
        copy = pltpu.make_async_remote_copy(
            src_ref=source,
            dst_ref=target,
            send_sem=send_sem,
            recv_sem=recv_sem,
            device_id=beside(lat, lon),
            device_id_type=MESH,
        )
        copy.start()
        return copy

    chunks = load_sem.shape[0]
    each = levels // chunks
    loads = [
        pltpu.make_async_copy(
            background.at[:, pl.ds(c * each, each)],
            held.at[:, pl.ds(c * each, each)],
            load_sem.at[c],
        )
        for c in range(chunks)
    ]
    for load in loads:
        load.start()
    lines = (level_in, row_in, col_in, frac_row_in, frac_col_in, value_in, error_in, flag_in)
    lines_held = (level, row, col, frac_row, frac_col, value, error, flag)
    line_loads = [
        pltpu.make_async_copy(there, here, line_sem.at[i])
        for i, (there, here) in enumerate(zip(lines, lines_held))
    ]
    for load in line_loads:
        load.start()

    around = [(lat, lon) for lat in SHIFTS for lon in SHIFTS if lat != 0 or lon != 0]
    barrier = pltpu.get_barrier_semaphore()
    for lat, lon in around:
        pl.semaphore_signal(barrier, inc=1, device_id=beside(lat, lon), device_id_type=MESH)
    pl.semaphore_wait(barrier, len(around))

    def place(pair, level):
        return pl.multiple_of((pair * levels + level) * stride + first, 8)

    def turned(upper, lower):
        return jnp.concatenate([upper, lower], axis=0).astype(bf16).T.astype(f32)

    def build(level, carry):
        stage[...] = held[:, level].astype(f32).reshape(members * depth, width)
        rows = [stage[pl.ds(r, members, stride=depth), :] for r in range(depth)]
        here = pl.ds(pl.multiple_of(level * members, members), members)
        edge[0, here, :] = rows[0].astype(bf16)
        edge[1, here, :] = rows[depth - 1].astype(bf16)
        for pair in range(1, depth):
            table[pl.ds(place(pair, level), width), :] = turned(rows[pair - 1], rows[pair])
        return carry

    part = each * members
    edge_copies = []
    for c in range(chunks):
        loads[c].wait()
        lax.fori_loop(c * each, (c + 1) * each, build, 0)
        span = pl.ds(c * part, part)
        edge_copies.append(
            [
                send(
                    edge.at[e, span],
                    edge_in.at[1 - e, span],
                    edge_send.at[e, c],
                    edge_recv.at[1 - e, c],
                    toward,
                    0,
                )
                for e, toward in ((0, -1), (1, 1))
            ]
        )

    inner = (depth - 1) * levels
    below = depth * levels * stride
    side_copies = []
    for s, toward in ((0, -1), (1, 1)):
        start = levels * stride + first + s * (width - 1)
        side[s] = table[pl.ds(start, inner, stride=stride), :].astype(bf16)
        for e, away in ((0, -1), (1, 1)):
            side_copies.append(
                send(
                    side.at[s, pl.ds(e * (inner - levels), levels)],
                    corner_in.at[1 - e, 1 - s],
                    corner_send.at[e, s],
                    corner_recv.at[1 - e, 1 - s],
                    away,
                    toward,
                )
            )
        side_copies.append(
            send(side.at[s], side_in.at[1 - s], side_send.at[s], side_recv.at[1 - s], 0, toward)
        )

    for load in line_loads:
        load.wait()
    spots[...] = (row[...] * levels + level[...]) * stride + (first - 1) + col[...]
    spot_load = pltpu.make_async_copy(spots, spot, spot_sem)
    spot_load.start()

    top = jnp.where(at_lat > 0, 1.0, 0.0).astype(f32)
    bottom = jnp.where(at_lat < n_lat - 1, 1.0, 0.0).astype(f32)

    def build_edges(level, carry):
        here = pl.ds(pl.multiple_of(level * members, members), members)
        north = edge_in[0, here, :].astype(f32) * top
        south = edge_in[1, here, :].astype(f32) * bottom
        table[pl.ds(place(0, level), width), :] = turned(north, edge[0, here, :].astype(f32))
        table[pl.ds(place(depth, level), width), :] = turned(edge[1, here, :].astype(f32), south)
        return carry

    for c in range(chunks):
        for copy in edge_copies[c]:
            copy.wait()
        lax.fori_loop(c * each, (c + 1) * each, build_edges, 0, unroll=each)
    spot_load.wait()
    for copy in side_copies:
        copy.wait()
    late = iota((levels, 2 * members), 1) >= members

    def swapped(x):
        return jnp.concatenate([x[:, members:], x[:, :members]], axis=1)

    for s in range(2):
        start = first - 1 + s * (width + 1)
        inside = side_in[s].astype(f32)
        above = jnp.where(late, corner_in[0, s].astype(f32) * top, inside[:levels])
        under = jnp.where(late, inside[inner - levels :], corner_in[1, s].astype(f32) * bottom)
        table[pl.ds(levels * stride + start, inner, stride=stride), :] = inside
        table[pl.ds(start, levels, stride=stride), :] = swapped(above)
        table[pl.ds(below + start, levels, stride=stride), :] = swapped(under)

    def pick(o, carry):
        picked[pl.ds(o * 2, 2), :] = table[pl.ds(spot[0, o], 2), :]
        return carry

    lax.fori_loop(0, observations, pick, 0, unroll=16)

    pert[members:, :] = jnp.zeros((pert.shape[0] - members, observations), bf16)
    lanes = 128

    def block(b, carry):
        start = pl.multiple_of(b * lanes, lanes)
        here = pl.ds(start, lanes)
        corners = [
            picked[pl.ds(start * 2 + s, lanes, stride=2), :].astype(bf16).T.astype(f32)
            for s in range(2)
        ]
        fr, fc = frac_row[:, here], frac_col[:, here]
        model = (
            (1.0 - fr) * (1.0 - fc) * corners[0][:members]
            + (1.0 - fr) * fc * corners[1][:members]
            + fr * (1.0 - fc) * corners[0][members:]
            + fr * fc * corners[1][members:]
        )
        mean = jnp.sum(model, axis=0, keepdims=True) * (1.0 / members)
        rounded = (model - mean).astype(bf16)
        pert[:members, here] = rounded
        innov = value[:, here] - mean
        flags = flag[:, here].astype(f32)
        departure[:, here] = flags * innov
        pert[members : members + 16, here] = jnp.where(iota((16, lanes), 0) == 0, innov, 0.0).astype(
            bf16
        )
        gain = (flags / error[:, here]).astype(bf16).astype(f32)
        along = (col[:, here].astype(f32) - 0.5 + fc - width / 2).astype(bf16).astype(f32)
        across = (row[:, here].astype(f32) - 0.5 + fr - depth / 2).astype(bf16).astype(f32)
        values = rounded.astype(f32)
        for a in range(3):
            u = (along - SHIFTS[a] * width) / width
            for c in range(3):
                w = (across - SHIFTS[c] * depth) / depth
                weight = gain * jnp.exp(-0.5 * (u * u + w * w))
                weighted[a, c * members : (c + 1) * members, here] = (values * weight).astype(bf16)
        return carry

    lax.fori_loop(0, observations // lanes, block, 0, unroll=2)

    sums_copies = []
    for a in (0, 2, 1):
        own[a] = dot_t(weighted[a], pert[...])
        for c in (0, 2, 1):
            if a != 1 or c != 1:
                sums_copies.append(
                    send(
                        own.at[a, pl.ds(c * members, members)],
                        sums_in.at[a, c],
                        sums_send.at[a, c],
                        sums_recv.at[a, c],
                        SHIFTS[c],
                        SHIFTS[a],
                    )
                )
    for copy in sums_copies:
        copy.wait()
    from_north = sums_in[0, 2] + sums_in[1, 2] + sums_in[2, 2]
    from_south = sums_in[0, 0] + sums_in[1, 0] + sums_in[2, 0]
    level_with = own[1, members : 2 * members, :] + sums_in[0, 1] + sums_in[2, 1]
    sums_out[...] = level_with + from_north * top + from_south * bottom


def transform_of(sums, members):
    eye = (iota((members, members), 0) == iota((members, members), 1)).astype(f32)
    system = (members - 1) / INFLATION * eye + sums[:, :members]
    squares = jnp.sum(system * system, axis=0, keepdims=True)
    scale = jnp.sqrt(jnp.sum(squares, axis=1, keepdims=True))
    upper = system / scale
    middle = 1.5 * eye - 0.5 * upper
    both = jnp.concatenate([dot(upper, middle), middle], axis=0)
    for step in range(1, NS_ITERS):
        middle = 1.5 * eye - 0.5 * dot(both[members:], both[:members])
        if step < NS_ITERS - 1:
            both = dot(both, middle)
        else:
            lower = dot(both[members:], middle)
    root = lower / jnp.sqrt(scale)
    mean_weights = dot(root, dot(root, sums))[:, members : members + 1]
    return (math.sqrt(members - 1) * root + mean_weights).astype(bf16)


def update(
    sums, ocean, departure, background, analysis, departure_out, held, result, spread_by, load_sem, store_sem
):
    members, levels, depth, width = background.shape
    half = 8
    halves = depth // half
    n = members * half
    chunks = load_sem.shape[0]
    each = members // chunks
    loads = [
        pltpu.make_async_copy(
            background.at[pl.ds(c * each, each)], held.at[pl.ds(c * each, each)], load_sem.at[c]
        )
        for c in range(chunks)
    ]
    for load in loads:
        load.start()
    departure_out[...] = departure[...]
    transform = transform_of(sums[...], members)
    shift = half.bit_length() - 1
    down = (jnp.right_shift(iota((n, members), 0), shift) == iota((n, members), 1)).astype(f32)
    along = (jnp.right_shift(iota((members, n), 1), shift) == iota((members, n), 0)).astype(f32)
    tall = dot_t(down.astype(bf16), transform).astype(bf16)
    wide = jnp.dot(tall, along.astype(bf16), preferred_element_type=f32)
    same = jnp.bitwise_and(iota((n, n), 0) - iota((n, n), 1), half - 1) == 0
    spread_by[...] = jnp.where(same, wide, 0.0).astype(bf16)
    for load in loads:
        load.wait()
    water = ocean[...] > 0
    at_once = 2

    def store(step):
        span = pl.ds(step * at_once, at_once)
        return pltpu.make_async_copy(result.at[:, span], analysis.at[:, span], store_sem.at[step])

    def one_level(level):
        state = held[:, level].astype(f32)
        mean = jnp.sum(state, axis=0) * (1.0 / members)
        spread = state - mean[None]
        spread = jnp.concatenate(
            [
                spread[:, h * half : (h + 1) * half].reshape(n, width).astype(bf16)
                for h in range(halves)
            ],
            axis=1,
        )
        mixed = jnp.dot(spread_by[...], spread, preferred_element_type=f32)
        change = jnp.concatenate(
            [
                mixed[:, h * width : (h + 1) * width].reshape(members, half, width)
                for h in range(halves)
            ],
            axis=1,
        )
        result[:, level] = jnp.where(
            water[None], mean[None] + change, held[:, level].astype(f32)
        ).astype(bf16)

    def some_levels(step, carry):
        for j in range(at_once):
            one_level(step * at_once + j)
        store(step).start()
        return carry

    lax.fori_loop(0, levels // at_once, some_levels, 0, unroll=2)
    for step in range(levels // at_once):
        store(step).wait()


def on_device(
    n_lon,
    n_lat,
    background,
    ocean,
    obs_level,
    obs_row,
    obs_col,
    frac_row,
    frac_col,
    obs_value,
    obs_error,
    obs_flag,
):
    members, levels, depth, width = background.shape
    observations = obs_level.shape[-1]
    stride = width + 8
    total = (depth + 1) * levels
    inner = (depth - 1) * levels
    chunks = math.gcd(levels, 8)
    lines = [
        x.reshape(1, observations)
        for x in (obs_level, obs_row, obs_col, frac_row, frac_col, obs_value, obs_error, obs_flag)
    ]
    vmem = pl.BlockSpec(memory_space=pltpu.VMEM)
    anywhere = pl.BlockSpec(memory_space=pl.ANY)
    dma = pltpu.SemaphoreType.DMA
    sums, departure = pl.pallas_call(
        functools.partial(observe, n_lon, n_lat),
        out_shape=(
            jax.ShapeDtypeStruct((members, 128), f32),
            jax.ShapeDtypeStruct((1, observations), f32),
        ),
        in_specs=[anywhere] * 9,
        out_specs=(vmem, vmem),
        scratch_shapes=[pltpu.VMEM(line.shape, line.dtype) for line in lines]
        + [
            pltpu.VMEM((1, observations), jnp.int32),
            pltpu.VMEM(background.shape, bf16),
            pltpu.VMEM((members * depth, width), f32),
            pltpu.VMEM((2, levels * members, width), bf16),
            pltpu.VMEM((2, levels * members, width), bf16),
            pltpu.VMEM((total * stride + 8, 2 * members), f32),
            pltpu.VMEM((2, inner, 2 * members), bf16),
            pltpu.VMEM((2, inner, 2 * members), bf16),
            pltpu.VMEM((2, 2, levels, 2 * members), bf16),
            pltpu.SMEM((1, observations), jnp.int32),
            pltpu.VMEM((2 * observations, 2 * members), f32),
            pltpu.VMEM((128, observations), bf16),
            pltpu.VMEM((3, 3 * members, observations), bf16),
            pltpu.VMEM((3, 3 * members, 128), f32),
            pltpu.VMEM((3, 3, members, 128), f32),
            dma((chunks,)),
            dma((8,)),
            dma,
            dma((2, chunks)),
            dma((2, chunks)),
            dma((2,)),
            dma((2,)),
            dma((2, 2)),
            dma((2, 2)),
            dma((3, 3)),
            dma((3, 3)),
        ],
        compiler_params=pltpu.CompilerParams(
            collective_id=0, has_side_effects=True, vmem_limit_bytes=48 << 20
        ),
        name="observe",
    )(background, *lines)
    n = members * 8
    analysis, departure = pl.pallas_call(
        update,
        out_shape=(
            jax.ShapeDtypeStruct(background.shape, bf16),
            jax.ShapeDtypeStruct(departure.shape, f32),
        ),
        in_specs=[vmem, vmem, vmem, anywhere],
        out_specs=(anywhere, vmem),
        scratch_shapes=[
            pltpu.VMEM(background.shape, bf16),
            pltpu.VMEM(background.shape, bf16),
            pltpu.VMEM((n, n), bf16),
            dma((8,)),
            dma((levels // 2,)),
        ],
        compiler_params=pltpu.CompilerParams(vmem_limit_bytes=40 << 20),
        name="update",
    )(sums, ocean, departure, background)
    return analysis, departure.reshape(obs_value.shape)


def solution(mesh):
    here = P("lat", "lon", None)
    in_specs = (P(None, None, "lat", "lon"), P("lat", "lon")) + (here,) * 8
    out_specs = (P(None, None, "lat", "lon"), here)
    return jax.shard_map(
        functools.partial(on_device, mesh.shape["lon"], mesh.shape["lat"]),
        mesh=mesh,
        in_specs=in_specs,
        out_specs=out_specs,
        check_vma=False,
    )
```

```python
import functools
import math

import jax
import jax.numpy as jnp
from jax import lax
from jax.experimental import pallas as pl
from jax.experimental.pallas import tpu as pltpu
from jax.sharding import PartitionSpec as P

NS_ITERS = 6
INFLATION = 1.2

f32 = jnp.float32
bf16 = jnp.bfloat16
MESH = pl.DeviceIdType.MESH
SHIFTS = (-1, 0, 1)


def iota(shape, axis):
    return lax.broadcasted_iota(jnp.int32, shape, axis)


def dot(a, b):
    return jnp.dot(a, b, precision=lax.Precision.HIGHEST, preferred_element_type=f32)


def dot_t(a, b):
    return lax.dot_general(a, b, (((1,), (1,)), ((), ())), preferred_element_type=f32)


def observe(
    n_lon,
    n_lat,
    background,
    level_in,
    row_in,
    col_in,
    frac_row_in,
    frac_col_in,
    value_in,
    error_in,
    flag_in,
    sums_out,
    departure,
    level,
    row,
    col,
    frac_row,
    frac_col,
    value,
    error,
    flag,
    spots,
    shares,
    held,
    stage,
    edge,
    edge_in,
    table,
    side,
    side_in,
    corner,
    corner_in,
    spot,
    picked,
    pert,
    weighted,
    own,
    sums_in,
    load_sem,
    line_sem,
    spot_sem,
    edge_send,
    edge_recv,
    side_send,
    side_recv,
    corner_send,
    corner_recv,
    sums_send,
    sums_recv,
):
    members, levels, depth, width = background.shape
    observations = spot.shape[1]
    stride = width + 8
    first = 8
    at_lon, at_lat = lax.axis_index("lon"), lax.axis_index("lat")

    def beside(lat, lon):
        return (lax.rem(at_lon + lon + n_lon, n_lon), lax.rem(at_lat + lat + n_lat, n_lat))

    def send(source, target, send_sem, recv_sem, lat, lon):
        copy = pltpu.make_async_remote_copy(
            src_ref=source,
            dst_ref=target,
            send_sem=send_sem,
            recv_sem=recv_sem,
            device_id=beside(lat, lon),
            device_id_type=MESH,
        )
        copy.start()
        return copy

    chunks = load_sem.shape[0]
    each = members // chunks
    loads = [
        pltpu.make_async_copy(
            background.at[pl.ds(c * each, each)], held.at[pl.ds(c * each, each)], load_sem.at[c]
        )
        for c in range(chunks)
    ]
    for load in loads:
        load.start()
    lines = (level_in, row_in, col_in, frac_row_in, frac_col_in, value_in, error_in, flag_in)
    lines_held = (level, row, col, frac_row, frac_col, value, error, flag)
    line_loads = [
        pltpu.make_async_copy(there, here, line_sem.at[i])
        for i, (there, here) in enumerate(zip(lines, lines_held))
    ]
    for load in line_loads:
        load.start()

    around = [(lat, lon) for lat in SHIFTS for lon in SHIFTS if lat != 0 or lon != 0]
    barrier = pltpu.get_barrier_semaphore()
    for lat, lon in around:
        pl.semaphore_signal(barrier, inc=1, device_id=beside(lat, lon), device_id_type=MESH)

    def place(pair, level):
        return pl.multiple_of((pair * levels + level) * stride + first, 8)

    def turned(upper, lower):
        return jnp.concatenate([upper, lower], axis=0).astype(bf16).T.astype(f32)

    def put(pair, level, upper, lower):
        table[pl.ds(place(pair, level), width), :] = turned(upper, lower)

    for c in range(chunks):
        loads[c].wait()

        def lay_out(level, carry):
            begin = c * each * depth
            some = held[c * each : (c + 1) * each, level].astype(f32)
            stage[level, begin : begin + each * depth, :] = some.reshape(each * depth, width)
            here = pl.ds(pl.multiple_of(level * members + c * each, each), each)
            for e in range(2):
                line = stage[level, pl.ds(begin + e * (depth - 1), each, stride=depth), :]
                edge[e, here, :] = line.astype(bf16)
            return carry

        lax.fori_loop(0, levels, lay_out, 0, unroll=4)

    pl.semaphore_wait(barrier, len(around))
    parts = edge_send.shape[1]
    part = levels // parts
    edge_copies = []
    for c in range(parts):
        span = pl.ds(c * part * members, part * members)
        edge_copies.append(
            [
                send(
                    edge.at[e, span],
                    edge_in.at[1 - e, span],
                    edge_send.at[e, c],
                    edge_recv.at[1 - e, c],
                    toward,
                    0,
                )
                for e, toward in ((0, -1), (1, 1))
            ]
        )

    def line_of(level, r):
        return stage[level, pl.ds(r, members, stride=depth), :]

    def build_outer(level, carry):
        put(1, level, line_of(level, 0), line_of(level, 1))
        put(depth - 1, level, line_of(level, depth - 2), line_of(level, depth - 1))
        return carry

    lax.fori_loop(0, levels, build_outer, 0, unroll=4)

    inner = (depth - 1) * levels
    below = depth * levels * stride
    side_copies = []
    for e, away in ((0, -1), (1, 1)):
        for s, toward in ((0, -1), (1, 1)):
            start = (levels + e * (inner - levels)) * stride + first + s * (width - 1)
            corner[e, s] = table[pl.ds(start, levels, stride=stride), :].astype(bf16)
            side_copies.append(
                send(
                    corner.at[e, s],
                    corner_in.at[1 - e, 1 - s],
                    corner_send.at[e, s],
                    corner_recv.at[1 - e, 1 - s],
                    away,
                    toward,
                )
            )

    def build(level, carry):
        rows = [line_of(level, r) for r in range(1, depth - 1)]
        for pair in range(2, depth - 1):
            put(pair, level, rows[pair - 2], rows[pair - 1])
        return carry

    lax.fori_loop(0, levels, build, 0, unroll=2)

    for s, toward in ((0, -1), (1, 1)):
        start = levels * stride + first + s * (width - 1)
        side[s] = table[pl.ds(start, inner, stride=stride), :].astype(bf16)
        side_copies.append(
            send(side.at[s], side_in.at[1 - s], side_send.at[s], side_recv.at[1 - s], 0, toward)
        )

    for load in line_loads:
        load.wait()
    spots[...] = (row[...] * levels + level[...]) * stride + (first - 1) + col[...]
    spot_load = pltpu.make_async_copy(spots, spot, spot_sem)
    spot_load.start()
    fr, fc = frac_row[...], frac_col[...]
    for k, share in enumerate(
        ((1.0 - fr) * (1.0 - fc), (1.0 - fr) * fc, fr * (1.0 - fc), fr * fc)
    ):
        shares[k : k + 1, :] = share
    flags = flag[...].astype(f32)
    gain = (flags / error[...]).astype(bf16).astype(f32)
    along = (col[...].astype(f32) - 0.5 + fc - width / 2).astype(bf16).astype(f32)
    across = (row[...].astype(f32) - 0.5 + fr - depth / 2).astype(bf16).astype(f32)
    for a in range(3):
        u = (along - SHIFTS[a] * width) / width
        for c in range(3):
            w = (across - SHIFTS[c] * depth) / depth
            k = 4 + a * 3 + c
            shares[k : k + 1, :] = gain * jnp.exp(-0.5 * (u * u + w * w))

    top = jnp.where(at_lat > 0, 1.0, 0.0).astype(f32)
    bottom = jnp.where(at_lat < n_lat - 1, 1.0, 0.0).astype(f32)

    def build_edges(level, carry):
        here = pl.ds(pl.multiple_of(level * members, members), members)
        north = edge_in[0, here, :].astype(f32) * top
        south = edge_in[1, here, :].astype(f32) * bottom
        put(0, level, north, line_of(level, 0))
        put(depth, level, line_of(level, depth - 1), south)
        return carry

    for c in range(parts):
        for copy in edge_copies[c]:
            copy.wait()
        lax.fori_loop(c * part, (c + 1) * part, build_edges, 0, unroll=part)
    spot_load.wait()
    for copy in side_copies:
        copy.wait()
    late = iota((levels, 2 * members), 1) >= members

    def swapped(x):
        return jnp.concatenate([x[:, members:], x[:, :members]], axis=1)

    for s in range(2):
        start = first - 1 + s * (width + 1)
        inside = side_in[s].astype(f32)
        above = jnp.where(late, corner_in[0, s].astype(f32) * top, inside[:levels])
        under = jnp.where(late, inside[inner - levels :], corner_in[1, s].astype(f32) * bottom)
        table[pl.ds(levels * stride + start, inner, stride=stride), :] = inside
        table[pl.ds(start, levels, stride=stride), :] = swapped(above)
        table[pl.ds(below + start, levels, stride=stride), :] = swapped(under)

    def pick(o, carry):
        picked[pl.ds(o * 2, 2), :] = table[pl.ds(spot[0, o], 2), :]
        return carry

    lax.fori_loop(0, observations, pick, 0, unroll=16)

    lanes = 128

    def block(b, carry):
        start = pl.multiple_of(b * lanes, lanes)
        here = pl.ds(start, lanes)
        left, right = (
            picked[pl.ds(start * 2 + s, lanes, stride=2), :].astype(bf16).T.astype(f32)
            for s in range(2)
        )
        model = (
            shares[0:1, here] * left[:members]
            + shares[1:2, here] * right[:members]
            + shares[2:3, here] * left[members:]
            + shares[3:4, here] * right[members:]
        )
        mean = jnp.sum(model, axis=0, keepdims=True) * (1.0 / members)
        rounded = (model - mean).astype(bf16)
        innov = value[:, here] - mean
        departure[:, here] = flag[:, here].astype(f32) * innov
        under = (lanes - members, lanes)
        under = jnp.where(iota(under, 0) == 0, innov, 0.0).astype(bf16)
        pert[here, :] = jnp.concatenate([rounded, under], axis=0).T
        values = rounded.astype(f32)
        for a in range(3):
            for c in range(3):
                k = 4 + a * 3 + c
                weighted[a, c * members : (c + 1) * members, here] = (
                    values * shares[k : k + 1, here]
                ).astype(bf16)
        return carry

    lax.fori_loop(0, observations // lanes, block, 0, unroll=2)

    sums_copies = []
    for a in (0, 2, 1):
        own[a] = jnp.dot(weighted[a], pert[...], preferred_element_type=f32)
        for c in (0, 2, 1):
            if a != 1 or c != 1:
                sums_copies.append(
                    send(
                        own.at[a, pl.ds(c * members, members)],
                        sums_in.at[a, c],
                        sums_send.at[a, c],
                        sums_recv.at[a, c],
                        SHIFTS[c],
                        SHIFTS[a],
                    )
                )
    for copy in sums_copies:
        copy.wait()
    from_north = sums_in[0, 2] + sums_in[1, 2] + sums_in[2, 2]
    from_south = sums_in[0, 0] + sums_in[1, 0] + sums_in[2, 0]
    level_with = own[1, members : 2 * members, :] + sums_in[0, 1] + sums_in[2, 1]
    sums_out[...] = level_with + from_north * top + from_south * bottom


def transform_of(sums, members):
    eye = (iota((members, members), 0) == iota((members, members), 1)).astype(f32)
    system = (members - 1) / INFLATION * eye + sums[:, :members]
    squares = jnp.sum(system * system, axis=0, keepdims=True)
    scale = jnp.sqrt(jnp.sum(squares, axis=1, keepdims=True))
    upper = system / scale
    middle = 1.5 * eye - 0.5 * upper
    both = jnp.concatenate([dot(upper, middle), middle], axis=0)
    for step in range(1, NS_ITERS):
        middle = 1.5 * eye - 0.5 * dot(both[members:], both[:members])
        if step < NS_ITERS - 1:
            both = dot(both, middle)
        else:
            lower = dot(both[members:], middle)
    root = lower / jnp.sqrt(scale)
    mean_weights = dot(root, dot(root, sums))[:, members : members + 1]
    return (math.sqrt(members - 1) * root + mean_weights).astype(bf16)


def update(
    sums, ocean, departure, background, analysis, departure_out, held, result, spread_by, load_sem, store_sem
):
    members, levels, depth, width = background.shape
    half = 8
    halves = depth // half
    n = members * half
    chunks = load_sem.shape[0]
    each = members // chunks
    loads = [
        pltpu.make_async_copy(
            background.at[pl.ds(c * each, each)], held.at[pl.ds(c * each, each)], load_sem.at[c]
        )
        for c in range(chunks)
    ]
    for load in loads:
        load.start()
    departure_out[...] = departure[...]
    transform = transform_of(sums[...], members)
    shift = half.bit_length() - 1
    down = (jnp.right_shift(iota((n, members), 0), shift) == iota((n, members), 1)).astype(f32)
    along = (jnp.right_shift(iota((members, n), 1), shift) == iota((members, n), 0)).astype(f32)
    tall = dot_t(down.astype(bf16), transform).astype(bf16)
    wide = jnp.dot(tall, along.astype(bf16), preferred_element_type=f32)
    same = jnp.bitwise_and(iota((n, n), 0) - iota((n, n), 1), half - 1) == 0
    spread_by[...] = jnp.where(same, wide, 0.0).astype(bf16)
    for load in loads:
        load.wait()
    water = ocean[...] > 0
    at_once = 2

    def store(step):
        span = pl.ds(step * at_once, at_once)
        return pltpu.make_async_copy(result.at[:, span], analysis.at[:, span], store_sem.at[step])

    def one_level(level):
        state = held[:, level].astype(f32)
        mean = jnp.sum(state, axis=0) * (1.0 / members)
        spread = state - mean[None]
        spread = jnp.concatenate(
            [
                spread[:, h * half : (h + 1) * half].reshape(n, width).astype(bf16)
                for h in range(halves)
            ],
            axis=1,
        )
        mixed = jnp.dot(spread_by[...], spread, preferred_element_type=f32)
        change = jnp.concatenate(
            [
                mixed[:, h * width : (h + 1) * width].reshape(members, half, width)
                for h in range(halves)
            ],
            axis=1,
        )
        result[:, level] = jnp.where(
            water[None], mean[None] + change, held[:, level].astype(f32)
        ).astype(bf16)

    def some_levels(step, carry):
        for j in range(at_once):
            one_level(step * at_once + j)
        store(step).start()
        return carry

    lax.fori_loop(0, levels // at_once, some_levels, 0, unroll=2)
    for step in range(levels // at_once):
        store(step).wait()


def on_device(
    n_lon,
    n_lat,
    background,
    ocean,
    obs_level,
    obs_row,
    obs_col,
    frac_row,
    frac_col,
    obs_value,
    obs_error,
    obs_flag,
):
    members, levels, depth, width = background.shape
    observations = obs_level.shape[-1]
    stride = width + 8
    total = (depth + 1) * levels
    inner = (depth - 1) * levels
    chunks, parts = 4, 4
    lines = [
        x.reshape(1, observations)
        for x in (obs_level, obs_row, obs_col, frac_row, frac_col, obs_value, obs_error, obs_flag)
    ]
    vmem = pl.BlockSpec(memory_space=pltpu.VMEM)
    outside = pl.BlockSpec(memory_space=pltpu.HBM)
    dma = pltpu.SemaphoreType.DMA
    sums, departure = pl.pallas_call(
        functools.partial(observe, n_lon, n_lat),
        out_shape=(
            jax.ShapeDtypeStruct((members, 128), f32),
            jax.ShapeDtypeStruct((1, observations), f32),
        ),
        in_specs=[outside] * 9,
        out_specs=(vmem, vmem),
        scratch_shapes=[pltpu.VMEM(line.shape, line.dtype) for line in lines]
        + [
            pltpu.VMEM((1, observations), jnp.int32),
            pltpu.VMEM((16, observations), f32),
            pltpu.VMEM(background.shape, bf16),
            pltpu.VMEM((levels, members * depth, width), f32),
            pltpu.VMEM((2, levels * members, width), bf16),
            pltpu.VMEM((2, levels * members, width), bf16),
            pltpu.VMEM((total * stride + 8, 2 * members), f32),
            pltpu.VMEM((2, inner, 2 * members), bf16),
            pltpu.VMEM((2, inner, 2 * members), bf16),
            pltpu.VMEM((2, 2, levels, 2 * members), bf16),
            pltpu.VMEM((2, 2, levels, 2 * members), bf16),
            pltpu.SMEM((1, observations), jnp.int32),
            pltpu.VMEM((2 * observations, 2 * members), f32),
            pltpu.VMEM((observations, 128), bf16),
            pltpu.VMEM((3, 3 * members, observations), bf16),
            pltpu.VMEM((3, 3 * members, 128), f32),
            pltpu.VMEM((3, 3, members, 128), f32),
            dma((chunks,)),
            dma((8,)),
            dma,
            dma((2, parts)),
            dma((2, parts)),
            dma((2,)),
            dma((2,)),
            dma((2, 2)),
            dma((2, 2)),
            dma((3, 3)),
            dma((3, 3)),
        ],
        compiler_params=pltpu.CompilerParams(
            collective_id=0, has_side_effects=True, vmem_limit_bytes=64 << 20
        ),
        name="observe",
    )(background, *lines)
    n = members * 8
    analysis, departure = pl.pallas_call(
        update,
        out_shape=(
            jax.ShapeDtypeStruct(background.shape, bf16),
            jax.ShapeDtypeStruct(departure.shape, f32),
        ),
        in_specs=[vmem, vmem, vmem, outside],
        out_specs=(outside, vmem),
        scratch_shapes=[
            pltpu.VMEM(background.shape, bf16),
            pltpu.VMEM(background.shape, bf16),
            pltpu.VMEM((n, n), bf16),
            dma((8,)),
            dma((levels // 2,)),
        ],
        compiler_params=pltpu.CompilerParams(vmem_limit_bytes=64 << 20),
        name="update",
    )(sums, ocean, departure, background)
    return analysis, departure.reshape(obs_value.shape)


def solution(mesh):
    here = P("lat", "lon", None)
    in_specs = (P(None, None, "lat", "lon"), P("lat", "lon")) + (here,) * 8
    out_specs = (P(None, None, "lat", "lon"), here)
    return jax.shard_map(
        functools.partial(on_device, mesh.shape["lon"], mesh.shape["lat"]),
        mesh=mesh,
        in_specs=in_specs,
        out_specs=out_specs,
        check_vma=False,
    )
```

```python
import functools
import math

import jax
import jax.numpy as jnp
from jax import lax
from jax.experimental import pallas as pl
from jax.experimental.pallas import tpu as pltpu
from jax.sharding import PartitionSpec as P

NS_ITERS = 6
INFLATION = 1.2

f32 = jnp.float32
bf16 = jnp.bfloat16
MESH = pl.DeviceIdType.MESH
SHIFTS = (-1, 0, 1)


def iota(shape, axis):
    return lax.broadcasted_iota(jnp.int32, shape, axis)


def dot(a, b):
    return jnp.dot(a, b, precision=lax.Precision.HIGHEST, preferred_element_type=f32)


def dot_t(a, b):
    return lax.dot_general(a, b, (((1,), (1,)), ((), ())), preferred_element_type=f32)


def observe(
    n_lon,
    n_lat,
    background,
    level_in,
    row_in,
    col_in,
    frac_row_in,
    frac_col_in,
    value_in,
    error_in,
    flag_in,
    sums_out,
    departure,
    level,
    row,
    col,
    frac_row,
    frac_col,
    value,
    error,
    flag,
    spots,
    shares,
    held,
    stage,
    edge,
    edge_in,
    table,
    side,
    side_in,
    corner,
    corner_in,
    spot,
    picked,
    pert,
    weighted,
    own,
    sums_in,
    load_sem,
    line_sem,
    spot_sem,
    edge_send,
    edge_recv,
    side_send,
    side_recv,
    corner_send,
    corner_recv,
    sums_send,
    sums_recv,
):
    members, levels, depth, width = background.shape
    observations = spot.shape[1]
    stride = width + 8
    first = 8
    at_lon, at_lat = lax.axis_index("lon"), lax.axis_index("lat")

    def beside(lat, lon):
        return (lax.rem(at_lon + lon + n_lon, n_lon), lax.rem(at_lat + lat + n_lat, n_lat))

    def send(source, target, send_sem, recv_sem, lat, lon):
        copy = pltpu.make_async_remote_copy(
            src_ref=source,
            dst_ref=target,
            send_sem=send_sem,
            recv_sem=recv_sem,
            device_id=beside(lat, lon),
            device_id_type=MESH,
        )
        copy.start()
        return copy

    chunks = load_sem.shape[0]
    each = members // chunks
    loads = [
        pltpu.make_async_copy(
            background.at[pl.ds(c * each, each)], held.at[pl.ds(c * each, each)], load_sem.at[c]
        )
        for c in range(chunks)
    ]
    for load in loads:
        load.start()
    lines = (level_in, row_in, col_in, frac_row_in, frac_col_in, value_in, error_in, flag_in)
    lines_held = (level, row, col, frac_row, frac_col, value, error, flag)
    line_loads = [
        pltpu.make_async_copy(there, here, line_sem.at[i])
        for i, (there, here) in enumerate(zip(lines, lines_held))
    ]
    for load in line_loads:
        load.start()

    around = [(lat, lon) for lat in SHIFTS for lon in SHIFTS if lat != 0 or lon != 0]
    barrier = pltpu.get_barrier_semaphore()
    for lat, lon in around:
        pl.semaphore_signal(barrier, inc=1, device_id=beside(lat, lon), device_id_type=MESH)

    def place(pair, level):
        return pl.multiple_of((pair * levels + level) * stride + first, 8)

    def turned(upper, lower):
        return jnp.concatenate([upper, lower], axis=0).astype(bf16).T.astype(f32)

    def put(pair, level, upper, lower):
        table[pl.ds(place(pair, level), width), :] = turned(upper, lower)

    for c in range(chunks):
        loads[c].wait()

        def lay_out(level, carry):
            begin = c * each * depth
            some = held[c * each : (c + 1) * each, level].astype(f32)
            stage[level, begin : begin + each * depth, :] = some.reshape(each * depth, width)
            here = pl.ds(pl.multiple_of(level * members + c * each, each), each)
            for e in range(2):
                line = stage[level, pl.ds(begin + e * (depth - 1), each, stride=depth), :]
                edge[e, here, :] = line.astype(bf16)
            return carry

        lax.fori_loop(0, levels, lay_out, 0, unroll=4)

    pl.semaphore_wait(barrier, len(around))
    parts = edge_send.shape[1]
    part = levels // parts
    edge_copies = []
    for c in range(parts):
        span = pl.ds(c * part * members, part * members)
        edge_copies.append(
            [
                send(
                    edge.at[e, span],
                    edge_in.at[1 - e, span],
                    edge_send.at[e, c],
                    edge_recv.at[1 - e, c],
                    toward,
                    0,
                )
                for e, toward in ((0, -1), (1, 1))
            ]
        )

    def line_of(level, r):
        return stage[level, pl.ds(r, members, stride=depth), :]

    def build_outer(level, carry):
        put(1, level, line_of(level, 0), line_of(level, 1))
        put(depth - 1, level, line_of(level, depth - 2), line_of(level, depth - 1))
        return carry

    lax.fori_loop(0, levels, build_outer, 0, unroll=4)

    inner = (depth - 1) * levels
    below = depth * levels * stride
    side_copies = []
    for e, away in ((0, -1), (1, 1)):
        for s, toward in ((0, -1), (1, 1)):
            start = (levels + e * (inner - levels)) * stride + first + s * (width - 1)
            corner[e, s] = table[pl.ds(start, levels, stride=stride), :].astype(bf16)
            side_copies.append(
                send(
                    corner.at[e, s],
                    corner_in.at[1 - e, 1 - s],
                    corner_send.at[e, s],
                    corner_recv.at[1 - e, 1 - s],
                    away,
                    toward,
                )
            )

    def build(level, carry):
        rows = [line_of(level, r) for r in range(1, depth - 1)]
        for pair in range(2, depth - 1):
            put(pair, level, rows[pair - 2], rows[pair - 1])
        return carry

    lax.fori_loop(0, levels, build, 0, unroll=2)

    for s, toward in ((0, -1), (1, 1)):
        start = levels * stride + first + s * (width - 1)
        side[s] = table[pl.ds(start, inner, stride=stride), :].astype(bf16)
        side_copies.append(
            send(side.at[s], side_in.at[1 - s], side_send.at[s], side_recv.at[1 - s], 0, toward)
        )

    for load in line_loads:
        load.wait()
    spots[...] = (row[...] * levels + level[...]) * stride + (first - 1) + col[...]
    spot_load = pltpu.make_async_copy(spots, spot, spot_sem)
    spot_load.start()
    fr, fc = frac_row[...], frac_col[...]
    for k, share in enumerate(
        ((1.0 - fr) * (1.0 - fc), (1.0 - fr) * fc, fr * (1.0 - fc), fr * fc)
    ):
        shares[k : k + 1, :] = share
    flags = flag[...].astype(f32)
    gain = (flags / error[...]).astype(bf16).astype(f32)
    along = (col[...].astype(f32) - 0.5 + fc - width / 2).astype(bf16).astype(f32)
    across = (row[...].astype(f32) - 0.5 + fr - depth / 2).astype(bf16).astype(f32)
    for a in range(3):
        u = (along - SHIFTS[a] * width) / width
        for c in range(3):
            w = (across - SHIFTS[c] * depth) / depth
            k = 4 + a * 3 + c
            shares[k : k + 1, :] = gain * jnp.exp(-0.5 * (u * u + w * w))

    top = jnp.where(at_lat > 0, 1.0, 0.0).astype(f32)
    bottom = jnp.where(at_lat < n_lat - 1, 1.0, 0.0).astype(f32)

    def build_edges(level, carry):
        here = pl.ds(pl.multiple_of(level * members, members), members)
        north = edge_in[0, here, :].astype(f32) * top
        south = edge_in[1, here, :].astype(f32) * bottom
        put(0, level, north, line_of(level, 0))
        put(depth, level, line_of(level, depth - 1), south)
        return carry

    for c in range(parts):
        for copy in edge_copies[c]:
            copy.wait()
        lax.fori_loop(c * part, (c + 1) * part, build_edges, 0, unroll=part)
    spot_load.wait()
    for copy in side_copies:
        copy.wait()
    late = iota((levels, 2 * members), 1) >= members

    def swapped(x):
        return jnp.concatenate([x[:, members:], x[:, :members]], axis=1)

    for s in range(2):
        start = first - 1 + s * (width + 1)
        inside = side_in[s].astype(f32)
        above = jnp.where(late, corner_in[0, s].astype(f32) * top, inside[:levels])
        under = jnp.where(late, inside[inner - levels :], corner_in[1, s].astype(f32) * bottom)
        table[pl.ds(levels * stride + start, inner, stride=stride), :] = inside
        table[pl.ds(start, levels, stride=stride), :] = swapped(above)
        table[pl.ds(below + start, levels, stride=stride), :] = swapped(under)

    def pick(o, carry):
        picked[pl.ds(o * 2, 2), :] = table[pl.ds(spot[0, o], 2), :]
        return carry

    lax.fori_loop(0, observations, pick, 0, unroll=16)

    lanes = 128

    def block(b, carry):
        start = pl.multiple_of(b * lanes, lanes)
        here = pl.ds(start, lanes)
        left, right = (
            picked[pl.ds(start * 2 + s, lanes, stride=2), :].astype(bf16).T.astype(f32)
            for s in range(2)
        )
        model = (
            shares[0:1, here] * left[:members]
            + shares[1:2, here] * right[:members]
            + shares[2:3, here] * left[members:]
            + shares[3:4, here] * right[members:]
        )
        mean = jnp.sum(model, axis=0, keepdims=True) * (1.0 / members)
        rounded = (model - mean).astype(bf16)
        innov = value[:, here] - mean
        departure[:, here] = flag[:, here].astype(f32) * innov
        under = (lanes - members, lanes)
        under = jnp.where(iota(under, 0) == 0, innov, 0.0).astype(bf16)
        pert[here, :] = jnp.concatenate([rounded, under], axis=0).T
        values = rounded.astype(f32)
        for a in range(3):
            for c in range(3):
                k = 4 + a * 3 + c
                weighted[a, c * members : (c + 1) * members, here] = (
                    values * shares[k : k + 1, here]
                ).astype(bf16)
        return carry

    lax.fori_loop(0, observations // lanes, block, 0, unroll=4)

    sums_copies = []
    for a in (0, 2, 1):
        own[a] = jnp.dot(weighted[a], pert[...], preferred_element_type=f32)
        for c in (0, 2, 1):
            if a != 1 or c != 1:
                sums_copies.append(
                    send(
                        own.at[a, pl.ds(c * members, members)],
                        sums_in.at[a, c],
                        sums_send.at[a, c],
                        sums_recv.at[a, c],
                        SHIFTS[c],
                        SHIFTS[a],
                    )
                )
    for copy in sums_copies:
        copy.wait()
    from_north = sums_in[0, 2] + sums_in[1, 2] + sums_in[2, 2]
    from_south = sums_in[0, 0] + sums_in[1, 0] + sums_in[2, 0]
    level_with = own[1, members : 2 * members, :] + sums_in[0, 1] + sums_in[2, 1]
    sums_out[...] = level_with + from_north * top + from_south * bottom


def transform_of(sums, members):
    eye = (iota((members, members), 0) == iota((members, members), 1)).astype(f32)
    system = (members - 1) / INFLATION * eye + sums[:, :members]
    squares = jnp.sum(system * system, axis=0, keepdims=True)
    scale = jnp.sqrt(jnp.sum(squares, axis=1, keepdims=True))
    upper = system / scale
    middle = 1.5 * eye - 0.5 * upper
    both = jnp.concatenate([dot(upper, middle), middle], axis=0)
    for step in range(1, NS_ITERS):
        middle = 1.5 * eye - 0.5 * dot(both[members:], both[:members])
        if step < NS_ITERS - 1:
            both = dot(both, middle)
        else:
            lower = dot(both[members:], middle)
    root = lower / jnp.sqrt(scale)
    mean_weights = dot(root, dot(root, sums))[:, members : members + 1]
    return (math.sqrt(members - 1) * root + mean_weights).astype(bf16)


def update(
    sums, ocean, departure, background, analysis, departure_out, held, result, spread_by, water_held, load_sem, store_sem, small_sem
):
    members, levels, depth, width = background.shape
    half = 8
    halves = depth // half
    n = members * half
    chunks = load_sem.shape[0]
    each = members // chunks
    loads = [
        pltpu.make_async_copy(
            background.at[pl.ds(c * each, each)], held.at[pl.ds(c * each, each)], load_sem.at[c]
        )
        for c in range(chunks)
    ]
    for load in loads:
        load.start()
    smalls = [
        pltpu.make_async_copy(ocean, water_held, small_sem.at[0]),
        pltpu.make_async_copy(departure, departure_out, small_sem.at[1]),
    ]
    for copy in smalls:
        copy.start()
    transform = transform_of(sums[...], members)
    shift = half.bit_length() - 1
    down = (jnp.right_shift(iota((n, members), 0), shift) == iota((n, members), 1)).astype(f32)
    along = (jnp.right_shift(iota((members, n), 1), shift) == iota((members, n), 0)).astype(f32)
    tall = dot_t(down.astype(bf16), transform).astype(bf16)
    wide = jnp.dot(tall, along.astype(bf16), preferred_element_type=f32)
    same = jnp.bitwise_and(iota((n, n), 0) - iota((n, n), 1), half - 1) == 0
    spread_by[...] = jnp.where(same, wide, 0.0).astype(bf16)
    for load in loads:
        load.wait()
    for copy in smalls:
        copy.wait()
    water = water_held[...] > 0
    at_once = 2

    def store(step):
        span = pl.ds(step * at_once, at_once)
        return pltpu.make_async_copy(result.at[:, span], analysis.at[:, span], store_sem.at[step])

    def one_level(level):
        state = held[:, level].astype(f32)
        mean = jnp.sum(state, axis=0) * (1.0 / members)
        spread = state - mean[None]
        spread = jnp.concatenate(
            [
                spread[:, h * half : (h + 1) * half].reshape(n, width).astype(bf16)
                for h in range(halves)
            ],
            axis=1,
        )
        mixed = jnp.dot(spread_by[...], spread, preferred_element_type=f32)
        change = jnp.concatenate(
            [
                mixed[:, h * width : (h + 1) * width].reshape(members, half, width)
                for h in range(halves)
            ],
            axis=1,
        )
        result[:, level] = jnp.where(
            water[None], mean[None] + change, held[:, level].astype(f32)
        ).astype(bf16)

    def some_levels(step, carry):
        for j in range(at_once):
            one_level(step * at_once + j)
        store(step).start()
        return carry

    lax.fori_loop(0, levels // at_once, some_levels, 0, unroll=2)
    for step in range(levels // at_once):
        store(step).wait()


def on_device(
    n_lon,
    n_lat,
    background,
    ocean,
    obs_level,
    obs_row,
    obs_col,
    frac_row,
    frac_col,
    obs_value,
    obs_error,
    obs_flag,
):
    members, levels, depth, width = background.shape
    observations = obs_level.shape[-1]
    stride = width + 8
    total = (depth + 1) * levels
    inner = (depth - 1) * levels
    chunks, parts = 4, 4
    lines = [
        x.reshape(1, observations)
        for x in (obs_level, obs_row, obs_col, frac_row, frac_col, obs_value, obs_error, obs_flag)
    ]
    vmem = pl.BlockSpec(memory_space=pltpu.VMEM)
    outside = pl.BlockSpec(memory_space=pltpu.HBM)
    dma = pltpu.SemaphoreType.DMA
    sums, departure = pl.pallas_call(
        functools.partial(observe, n_lon, n_lat),
        out_shape=(
            jax.ShapeDtypeStruct((members, 128), f32),
            jax.ShapeDtypeStruct((1, observations), f32),
        ),
        in_specs=[outside] * 9,
        out_specs=(vmem, vmem),
        scratch_shapes=[pltpu.VMEM(line.shape, line.dtype) for line in lines]
        + [
            pltpu.VMEM((1, observations), jnp.int32),
            pltpu.VMEM((16, observations), f32),
            pltpu.VMEM(background.shape, bf16),
            pltpu.VMEM((levels, members * depth, width), f32),
            pltpu.VMEM((2, levels * members, width), bf16),
            pltpu.VMEM((2, levels * members, width), bf16),
            pltpu.VMEM((total * stride + 8, 2 * members), f32),
            pltpu.VMEM((2, inner, 2 * members), bf16),
            pltpu.VMEM((2, inner, 2 * members), bf16),
            pltpu.VMEM((2, 2, levels, 2 * members), bf16),
            pltpu.VMEM((2, 2, levels, 2 * members), bf16),
            pltpu.SMEM((1, observations), jnp.int32),
            pltpu.VMEM((2 * observations, 2 * members), f32),
            pltpu.VMEM((observations, 128), bf16),
            pltpu.VMEM((3, 3 * members, observations), bf16),
            pltpu.VMEM((3, 3 * members, 128), f32),
            pltpu.VMEM((3, 3, members, 128), f32),
            dma((chunks,)),
            dma((8,)),
            dma,
            dma((2, parts)),
            dma((2, parts)),
            dma((2,)),
            dma((2,)),
            dma((2, 2)),
            dma((2, 2)),
            dma((3, 3)),
            dma((3, 3)),
        ],
        compiler_params=pltpu.CompilerParams(
            collective_id=0, has_side_effects=True, vmem_limit_bytes=64 << 20
        ),
        name="observe",
    )(background, *lines)
    n = members * 8
    analysis, departure = pl.pallas_call(
        update,
        out_shape=(
            jax.ShapeDtypeStruct(background.shape, bf16),
            jax.ShapeDtypeStruct(departure.shape, f32),
        ),
        in_specs=[vmem, outside, outside, outside],
        out_specs=(outside, outside),
        scratch_shapes=[
            pltpu.VMEM(background.shape, bf16),
            pltpu.VMEM(background.shape, bf16),
            pltpu.VMEM((n, n), bf16),
            pltpu.VMEM(ocean.shape, ocean.dtype),
            dma((8,)),
            dma((levels // 2,)),
            dma((2,)),
        ],
        compiler_params=pltpu.CompilerParams(vmem_limit_bytes=64 << 20),
        name="update",
    )(sums, ocean, departure, background)
    return analysis, departure.reshape(obs_value.shape)


def solution(mesh):
    here = P("lat", "lon", None)
    in_specs = (P(None, None, "lat", "lon"), P("lat", "lon")) + (here,) * 8
    out_specs = (P(None, None, "lat", "lon"), here)
    return jax.shard_map(
        functools.partial(on_device, mesh.shape["lon"], mesh.shape["lat"]),
        mesh=mesh,
        in_specs=in_specs,
        out_specs=out_specs,
        check_vma=False,
    )
```
